32 devices in a mesh: cuts: 4 (over z), amp: 8 (over y, x, core).
Axes of the slice: x: 2, y: 2, z: 4, core: 2. Of those that a mesh axis runs over, the one named last changes fastest.
Arguments:
- stem_state: bfloat16 [8, 32, 8, 128, 256], P('cuts', None, 'amp'), may hold values from -6 to 6
- gates: bfloat16 [8, 4, 2, 128, 128], P('cuts'), may hold values from -0.375 to 0.375
Outputs:
- amplitudes: float32 [32, 8, 128, 256], P('cuts', 'amp')
The draws below stay inside these ranges and needn't reach their ends.
All inputs are finite; a program needn't handle non-finite values.
Results may differ from the reference program's by a relative error of at most 0.0049.
Values may be sent and summed in bfloat16 or wider, within the bound.
A program may use at most 64 MiB of HBM per device.

```python
import jax
import jax.numpy as jnp
from jax import lax

G = 128
HI = 32
SLICES = 8
N_AMP = 8


def with_spikes(values, own_key, source, target, blocks, factor):
    owner, partner = [(jnp.arange(values.shape[axis_at]) // (values.shape[axis_at] // blocks)).reshape([-1 if axis == axis_at else 1 for axis in range(values.ndim)]) for axis_at in (source, target)]
    chosen = jax.random.permutation(own_key, blocks)[partner]
    strong = (owner == chosen) | (owner == (partner + blocks // 2) % blocks)
    return jnp.where(strong, factor * values, values)


def level_of(own_key, dims, shards, low, top_value):
    factor_of = 1.0
    for axis_at, parts in shards:
        draws = jax.random.uniform(jax.random.fold_in(jax.random.fold_in(own_key, 6), axis_at), (parts,), jnp.float32, low / len(shards), top_value / len(shards))
        factor_of = factor_of * jnp.repeat(jnp.exp(draws), dims[axis_at] // parts).reshape((-1,) + (1,) * (len(dims) - 1 - axis_at))
    return factor_of


def bell_draw(key, shape, scale, bound, pieces=(), kind=jnp.bfloat16):
    values = jax.random.normal(key, shape, jnp.float32) * scale
    if len(pieces) > 0:
        values = level_of(key, shape, pieces, -0.22, 0.18) * values
    return jnp.clip(values, min=-bound, max=bound).astype(kind)


def gaussian_with(rng, extent, spread, bound, pieces, heavy, held_as=jnp.bfloat16):
    drawn = spread * jax.random.normal(rng, extent, jnp.float32)
    if pieces:
        drawn = drawn * level_of(rng, extent, pieces, -0.22, 0.18)
    return jnp.clip(with_spikes(drawn, jax.random.fold_in(rng, 3), *heavy), -bound, bound).astype(held_as)


def setup_inputs(seed: int = 0) -> dict:
    streams_of = jax.random.split(jax.random.key(seed), 3)
    stem_state = gaussian_with(streams_of[0], (SLICES, HI, N_AMP, G, 2 * G), 1.0, 6.0, ((0, 4), (2, 8)), (0, 1, 4, 2.0))
    gates = bell_draw(streams_of[1], (SLICES, 4, 2, G, G), (2 * G) ** -0.5, 0.375, ((0, 4),))
    return {"stem_state": stem_state, "gates": gates}


def block_matrix(gate):
    real_part = gate[0]
    imag_part = gate[1]
    top = jnp.concatenate([real_part.T, imag_part.T], axis=1)
    bottom = jnp.concatenate([-imag_part.T, real_part.T], axis=1)
    return jnp.concatenate([top, bottom], axis=0)


def on_rows(values, gate):
    width = values.shape[-1] // 2
    real_part = gate[0].astype(jnp.float32)
    imag_part = gate[1].astype(jnp.float32)
    first_term = jnp.einsum('ka,...ac->...kc', real_part, values.astype(jnp.float32))
    second_term = jnp.einsum('ka,...ac->...kc', imag_part, values.astype(jnp.float32))
    real_out = first_term[..., :width] - second_term[..., width:]
    imag_out = first_term[..., width:] + second_term[..., :width]
    return jnp.concatenate([real_out, imag_out], axis=-1)


def on_last(values, gate):
    columns = values.shape[-1]
    flat = values.reshape(-1, columns)
    result = jnp.dot(flat, block_matrix(gate), preferred_element_type=jnp.float32)
    return result.reshape(values.shape)


def per_value(block, gates):
    groups = block.shape[0]
    width = block.shape[1]
    low = width // groups
    first = on_rows(block, gates[0]).astype(jnp.bfloat16)
    second = on_last(first, gates[1]).astype(jnp.bfloat16)
    moved = second.reshape(groups, groups, low, 2 * width)
    moved = jnp.transpose(moved, (1, 0, 2, 3)).reshape(groups, width, 2 * width)
    third = on_rows(moved, gates[2]).astype(jnp.bfloat16)
    fourth = on_last(third, gates[3])
    back = fourth.reshape(groups, groups, low, 2 * width)
    return jnp.transpose(back, (1, 0, 2, 3)).reshape(groups, width, 2 * width)


def reference(stem_state, gates):
    def add_slice(total, pair):
        state, slice_gates = pair
        result = lax.map(lambda block: per_value(block, slice_gates), state)
        return total + result, None

    start = jnp.zeros(stem_state.shape[1:], jnp.float32)
    total, unused = lax.scan(add_slice, start, (stem_state, gates))
    return total
```

```python
import functools

import jax
import jax.numpy as jnp
from jax import lax
from jax.experimental import pallas as pl
from jax.experimental.pallas import tpu as pltpu
from jax.sharding import PartitionSpec as P

MESH = pl.DeviceIdType.MESH
WINDOW = 2


def block_matrix(gate):
    real_part = gate[0]
    imag_part = gate[1]
    top = jnp.concatenate([real_part.T, imag_part.T], axis=1)
    bottom = jnp.concatenate([-imag_part.T, real_part.T], axis=1)
    return jnp.concatenate([top, bottom], axis=0)


def on_rows(values, real_gates, imag_gates):
    width = values.shape[-1] // 2
    first_term = jnp.einsum(
        "ska,shgac->shgkc", real_gates, values, preferred_element_type=jnp.float32
    )
    second_term = jnp.einsum(
        "ska,shgac->shgkc", imag_gates, values, preferred_element_type=jnp.float32
    )
    real_out = first_term[..., :width] - second_term[..., width:]
    imag_out = first_term[..., width:] + second_term[..., :width]
    return jnp.concatenate([real_out, imag_out], axis=-1)


def on_last(values, matrices):
    return jnp.einsum("shgac,scd->shgad", values, matrices, preferred_element_type=jnp.float32)


def per_device_general(stem_state, gates):
    groups = lax.axis_size("amp")
    slice_count, hidden, single, width, columns = stem_state.shape
    low = width // groups
    first = on_rows(stem_state, gates[:, 0, 0], gates[:, 0, 1]).astype(jnp.bfloat16)
    second_matrix = jax.vmap(block_matrix)(gates[:, 1])
    second = on_last(first, second_matrix).astype(jnp.bfloat16)
    split_state = second.reshape(slice_count, hidden, 1, groups, low, columns)
    last_matrix = jax.vmap(block_matrix)(gates[:, 3])
    pieces = lax.all_to_all(split_state, "amp", split_axis=3, concat_axis=2, tiled=True)
    count = pieces.shape[1]
    merged = pieces.reshape(slice_count, count, 1, width, columns)
    third = on_rows(merged, gates[:, 2, 0], gates[:, 2, 1]).astype(jnp.bfloat16)
    fourth = on_last(third, last_matrix).reshape(slice_count, count, width, columns)
    total = jnp.sum(fourth, axis=0)
    summed = lax.psum_scatter(total, "cuts", scatter_dimension=0, tiled=True)
    share = summed.shape[0]
    outgoing = summed.reshape(share, groups, 1, low, columns)
    owned = lax.all_to_all(outgoing, "amp", split_axis=1, concat_axis=2, tiled=True)
    return owned.reshape(share, 1, width, columns)


def dot(a, b):
    return jnp.dot(a, b, preferred_element_type=jnp.float32)


def pair_of(first, second):
    half = first.shape[1] // 2
    return jnp.concatenate(
        [
            jnp.concatenate([first[:, :half], second[:, :half]], axis=1),
            jnp.concatenate([first[:, half:], second[:, half:]], axis=1),
        ],
        axis=0,
    )


def kernel(cuts, groups, stem, gates, out, land, gate_buf, blocks, moved, parts, arrived, own,
           stage, in_send, in_recv, z_send, z_recv, back_send, back_recv, local_sem, gate_sem,
           own_sem):
    slices = stem.shape[0]
    width = stem.shape[3]
    columns = stem.shape[4]
    low = width // groups
    k = lax.axis_index("cuts")
    j = lax.axis_index("amp")

    barrier = pltpu.get_barrier_semaphore()
    for i in range(1, groups):
        pl.semaphore_signal(barrier, inc=1, device_id=(k, lax.rem(j + i, groups)), device_id_type=MESH)
    for i in range(1, cuts):
        pl.semaphore_signal(barrier, inc=1, device_id=(lax.rem(k + i, cuts), j), device_id_type=MESH)
    gate_copy = pltpu.make_async_copy(gates, gate_buf, gate_sem)
    gate_copy.start()

    half = k // 2
    order = [3 * (1 - half), 2 - half, 4 * half + 1 - k, k]

    def local_in(step):
        return pltpu.make_async_copy(
            stem.at[:, order[step] * groups + j, 0], land.at[step, :, j], local_sem.at[step]
        )

    def send_in(step, i):
        peer = lax.rem(j + i, groups)
        return pltpu.make_async_remote_copy(
            src_ref=stem.at[:, order[step] * groups + peer, 0],
            dst_ref=land.at[step, :, j],
            send_sem=in_send.at[step, i - 1],
            recv_sem=in_recv.at[step, i - 1],
            device_id=(k, peer),
            device_id_type=MESH,
        )

    def arrive_in(step, i):
        peer = lax.rem(j + groups - i, groups)
        return pltpu.make_async_remote_copy(
            src_ref=land.at[step, :, peer],
            dst_ref=land.at[step, :, peer],
            send_sem=in_send.at[step, i - 1],
            recv_sem=in_recv.at[step, i - 1],
            device_id=(k, peer),
            device_id_type=MESH,
        )

    def issue(step):
        for i in range(1, groups):
            send_in(step, i).start()

    for step in range(cuts):
        local_in(step).start()
    pl.semaphore_wait(barrier, groups - 1 + cuts - 1)
    for step in range(WINDOW):
        issue(step)

    gate_copy.wait()
    for s in range(slices):
        for n in range(4):
            re = gate_buf[s, n, 0]
            im = gate_buf[s, n, 1]
            if n % 2 == 0:
                blocks[s, n, :width, :width] = re
                blocks[s, n, :width, width:] = -im
                blocks[s, n, width:, :width] = im
                blocks[s, n, width:, width:] = re
            else:
                re = re.T
                im = im.T
                blocks[s, n, :width, :width] = re
                blocks[s, n, :width, width:] = im
                blocks[s, n, width:, :width] = -im
                blocks[s, n, width:, width:] = re

    def rows_then_last(pair, s, n):
        mid = dot(blocks[s, n], pair).astype(jnp.bfloat16)
        turned = jnp.concatenate(
            [
                jnp.concatenate([mid[:width, :width], mid[width:, :width]], axis=1),
                jnp.concatenate([mid[:width, width:], mid[width:, width:]], axis=1),
            ],
            axis=0,
        )
        return dot(turned, blocks[s, n + 1])

    def compute(step, write):
        for s in range(slices):
            @pl.loop(0, groups // 2)
            def _(m, s=s):
                g = 2 * m
                res = rows_then_last(
                    pair_of(land[step, s, g], land[step, s, g + 1]), s, 0
                ).astype(jnp.bfloat16)
                for d in range(2):
                    for p in range(groups):
                        moved[s, p, pl.ds(pl.multiple_of((g + d) * low, low), low), :] = (
                            res[d * width + p * low : d * width + (p + 1) * low]
                        )

        @pl.loop(0, groups // 2)
        def _(m):
            p = 2 * m
            total = None
            for s in range(slices):
                term = rows_then_last(pair_of(moved[s, p], moved[s, p + 1]), s, 2)
                total = term if total is None else total + term
            for d in range(2):
                for g in range(groups):
                    write(g, p + d, total[d * width + g * low : d * width + (g + 1) * low])

    def z_copy(step):
        slot = lax.rem(k - order[step] + cuts - 1, cuts)
        return pltpu.make_async_remote_copy(
            src_ref=parts.at[step],
            dst_ref=arrived.at[slot],
            send_sem=z_send.at[step],
            recv_sem=z_recv.at[slot],
            device_id=(order[step], j),
            device_id_type=MESH,
        )

    for step in range(cuts):
        local_in(step).wait()
        for i in range(1, groups):
            arrive_in(step, i).wait_recv()
        if step + WINDOW < cuts:
            for i in range(1, groups):
                send_in(step, i).wait_send()
            issue(step + WINDOW)
        if step < cuts - 1:
            def write(g, p, rows, step=step):
                parts[step, g, pl.ds(pl.multiple_of(p * low, low), low), :] = rows.astype(jnp.bfloat16)
        else:
            def write(g, p, rows):
                own[g, pl.ds(pl.multiple_of(p * low, low), low), :] = rows
        compute(step, write)
        if step < cuts - 1:
            z_copy(step).start()

    for slot in range(cuts - 1):
        pltpu.make_async_remote_copy(
            src_ref=arrived.at[slot],
            dst_ref=arrived.at[slot],
            send_sem=z_send.at[slot],
            recv_sem=z_recv.at[slot],
            device_id=(lax.rem(k + slot + 1, cuts), j),
            device_id_type=MESH,
        ).wait_recv()

    def back(i):
        peer = lax.rem(j + i, groups)
        return pltpu.make_async_remote_copy(
            src_ref=stage.at[peer],
            dst_ref=out.at[j],
            send_sem=back_send.at[i - 1],
            recv_sem=back_recv.at[i - 1],
            device_id=(k, peer),
            device_id_type=MESH,
        )

    own_copy = pltpu.make_async_copy(stage.at[j], out.at[j], own_sem)
    for i in list(range(1, groups)) + [0]:
        peer = lax.rem(j + i, groups)
        total = own[peer]
        for slot in range(cuts - 1):
            total = total + arrived[slot, peer].astype(jnp.float32)
        stage[peer] = total.astype(jnp.bfloat16)
        if i > 0:
            back(i).start()
        else:
            own_copy.start()

    for step in range(max(cuts - WINDOW, 0), cuts):
        for i in range(1, groups):
            send_in(step, i).wait_send()
    for step in range(cuts - 1):
        z_copy(step).wait_send()
    for i in range(1, groups):
        back(i).wait_send()
    for i in range(1, groups):
        peer = lax.rem(j + groups - i, groups)
        pltpu.make_async_remote_copy(
            src_ref=stage.at[peer],
            dst_ref=out.at[peer],
            send_sem=back_send.at[i - 1],
            recv_sem=back_recv.at[i - 1],
            device_id=(k, peer),
            device_id_type=MESH,
        ).wait_recv()
    own_copy.wait()


def per_device_fused(stem_state, gates):
    cuts = lax.axis_size("cuts")
    groups = lax.axis_size("amp")
    slices, hidden, single, width, columns = stem_state.shape
    state = (groups, width, columns)
    bf16 = jnp.bfloat16
    result = pl.pallas_call(
        functools.partial(kernel, cuts, groups),
        out_shape=jax.ShapeDtypeStruct(state, bf16),
        in_specs=[pl.BlockSpec(memory_space=pl.ANY)] * 2,
        out_specs=pl.BlockSpec(memory_space=pl.ANY),
        scratch_shapes=[
            pltpu.VMEM((cuts, slices) + state, bf16),
            pltpu.VMEM(gates.shape, bf16),
            pltpu.VMEM((slices, 4, columns, columns), bf16),
            pltpu.VMEM((slices,) + state, bf16),
            pltpu.VMEM((cuts - 1,) + state, bf16),
            pltpu.VMEM((cuts - 1,) + state, bf16),
            pltpu.VMEM(state, jnp.float32),
            pltpu.VMEM(state, bf16),
            pltpu.SemaphoreType.DMA((cuts, groups - 1)),
            pltpu.SemaphoreType.DMA((cuts, groups - 1)),
            pltpu.SemaphoreType.DMA((cuts - 1,)),
            pltpu.SemaphoreType.DMA((cuts - 1,)),
            pltpu.SemaphoreType.DMA((groups - 1,)),
            pltpu.SemaphoreType.DMA((groups - 1,)),
            pltpu.SemaphoreType.DMA((cuts,)),
            pltpu.SemaphoreType.DMA,
            pltpu.SemaphoreType.DMA,
        ],
        compiler_params=pltpu.CompilerParams(
            collective_id=0, has_side_effects=True, vmem_limit_bytes=40 * 1024 * 1024
        ),
    )(stem_state, gates)
    return result.astype(jnp.float32).reshape(hidden // cuts, 1, width, columns)


def per_device(stem_state, gates):
    cuts = lax.axis_size("cuts")
    groups = lax.axis_size("amp")
    hidden, width = stem_state.shape[1], stem_state.shape[3]
    if cuts == 4 and hidden == cuts * groups and width % (16 * groups) == 0 and groups % 2 == 0:
        return per_device_fused(stem_state, gates)
    return per_device_general(stem_state, gates)


def solution(mesh):
    placed = (P("cuts", None, "amp", None, None), P("cuts", None, None, None, None))
    return jax.shard_map(
        per_device,
        mesh=mesh,
        in_specs=placed,
        out_specs=P("cuts", "amp", None, None),
        check_vma=False,
    )
```

```python
import functools

import jax
import jax.numpy as jnp
from jax import lax
from jax.experimental import pallas as pl
from jax.experimental.pallas import tpu as pltpu
from jax.sharding import PartitionSpec as P

MESH = pl.DeviceIdType.MESH


def block_matrix(gate):
    real_part = gate[0]
    imag_part = gate[1]
    top = jnp.concatenate([real_part.T, imag_part.T], axis=1)
    bottom = jnp.concatenate([-imag_part.T, real_part.T], axis=1)
    return jnp.concatenate([top, bottom], axis=0)


def on_rows(values, real_gates, imag_gates):
    width = values.shape[-1] // 2
    first_term = jnp.einsum(
        "ska,shgac->shgkc", real_gates, values, preferred_element_type=jnp.float32
    )
    second_term = jnp.einsum(
        "ska,shgac->shgkc", imag_gates, values, preferred_element_type=jnp.float32
    )
    real_out = first_term[..., :width] - second_term[..., width:]
    imag_out = first_term[..., width:] + second_term[..., :width]
    return jnp.concatenate([real_out, imag_out], axis=-1)


def on_last(values, matrices):
    return jnp.einsum("shgac,scd->shgad", values, matrices, preferred_element_type=jnp.float32)


def per_device_general(stem_state, gates):
    groups = lax.axis_size("amp")
    slice_count, hidden, single, width, columns = stem_state.shape
    low = width // groups
    first = on_rows(stem_state, gates[:, 0, 0], gates[:, 0, 1]).astype(jnp.bfloat16)
    second_matrix = jax.vmap(block_matrix)(gates[:, 1])
    second = on_last(first, second_matrix).astype(jnp.bfloat16)
    split_state = second.reshape(slice_count, hidden, 1, groups, low, columns)
    last_matrix = jax.vmap(block_matrix)(gates[:, 3])
    pieces = lax.all_to_all(split_state, "amp", split_axis=3, concat_axis=2, tiled=True)
    count = pieces.shape[1]
    merged = pieces.reshape(slice_count, count, 1, width, columns)
    third = on_rows(merged, gates[:, 2, 0], gates[:, 2, 1]).astype(jnp.bfloat16)
    fourth = on_last(third, last_matrix).reshape(slice_count, count, width, columns)
    total = jnp.sum(fourth, axis=0)
    summed = lax.psum_scatter(total, "cuts", scatter_dimension=0, tiled=True)
    share = summed.shape[0]
    outgoing = summed.reshape(share, groups, 1, low, columns)
    owned = lax.all_to_all(outgoing, "amp", split_axis=1, concat_axis=2, tiled=True)
    return owned.reshape(share, 1, width, columns)


def dot(a, b):
    return jnp.dot(a, b, preferred_element_type=jnp.float32)


def pair_of(first, second):
    half = first.shape[1] // 2
    return jnp.concatenate(
        [
            jnp.concatenate([first[:, :half], second[:, :half]], axis=1),
            jnp.concatenate([first[:, half:], second[:, half:]], axis=1),
        ],
        axis=0,
    )


def kernel(cuts, groups, stem, gates, out, land, gate_buf, blocks, moved, parts, slots, own,
           stage, in_send, in_recv, z_send, z_recv, back_send, back_recv, local_sem, gate_sem,
           own_sem):
    slices = stem.shape[0]
    width = stem.shape[3]
    low = width // groups
    k = lax.axis_index("cuts")
    j = lax.axis_index("amp")

    barrier = pltpu.get_barrier_semaphore()
    for i in range(1, groups):
        pl.semaphore_signal(barrier, inc=1, device_id=(k, lax.rem(j + i, groups)), device_id_type=MESH)
    for i in range(1, cuts):
        pl.semaphore_signal(barrier, inc=1, device_id=(lax.rem(k + i, cuts), j), device_id_type=MESH)
    gate_copy = pltpu.make_async_copy(gates, gate_buf, gate_sem)
    gate_copy.start()

    half = k // 2
    inner = (k * (3 - k)) // 2
    outer = 1 - inner
    order = [3 * (1 - half), 2 - half, 4 * half + 1 - k, k]

    def local_in(step, s):
        return pltpu.make_async_copy(
            stem.at[s, order[step] * groups + j, 0], land.at[step, s, j], local_sem.at[step, s]
        )

    def send_in(step, s, i):
        peer = lax.rem(j + i, groups)
        return pltpu.make_async_remote_copy(
            src_ref=stem.at[s, order[step] * groups + peer, 0],
            dst_ref=land.at[step, s, j],
            send_sem=in_send.at[step, s, i - 1],
            recv_sem=in_recv.at[step, s, i - 1],
            device_id=(k, peer),
            device_id_type=MESH,
        )

    def arrive_in(step, s, i):
        peer = lax.rem(j + groups - i, groups)
        return pltpu.make_async_remote_copy(
            src_ref=land.at[step, s, peer],
            dst_ref=land.at[step, s, peer],
            send_sem=in_send.at[step, s, i - 1],
            recv_sem=in_recv.at[step, s, i - 1],
            device_id=(k, peer),
            device_id_type=MESH,
        )

    pl.semaphore_wait(barrier, groups - 1 + cuts - 1)
    for step in range(cuts):
        for s in range(slices):
            for i in range(1, groups):
                send_in(step, s, i).start()
            local_in(step, s).start()

    gate_copy.wait()
    for s in range(slices):
        for n in range(4):
            re = gate_buf[s, n, 0]
            im = gate_buf[s, n, 1]
            if n % 2 == 0:
                blocks[s, n, :width, :width] = re
                blocks[s, n, :width, width:] = -im
                blocks[s, n, width:, :width] = im
                blocks[s, n, width:, width:] = re
            else:
                re = re.T
                im = im.T
                blocks[s, n, :width, :width] = re
                blocks[s, n, :width, width:] = im
                blocks[s, n, width:, :width] = -im
                blocks[s, n, width:, width:] = re

    def rows_then_last(pair, s, n):
        mid = dot(blocks[s, n], pair).astype(jnp.bfloat16)
        turned = jnp.concatenate(
            [
                jnp.concatenate([mid[:width, :width], mid[width:, :width]], axis=1),
                jnp.concatenate([mid[:width, width:], mid[width:, width:]], axis=1),
            ],
            axis=0,
        )
        return dot(turned, blocks[s, n + 1])

    def first_two(step, s):
        @pl.loop(0, groups // 2)
        def _(m):
            g = 2 * m
            res = rows_then_last(
                pair_of(land[step, s, g], land[step, s, g + 1]), s, 0
            ).astype(jnp.bfloat16)
            for d in range(2):
                for p in range(groups):
                    moved[p, pl.ds(pl.multiple_of((g + d) * low, low), low), :] = (
                        res[d * width + p * low : d * width + (p + 1) * low]
                    )

    def last_two(s, start, stop, write):
        @pl.loop(start, stop)
        def _(m):
            p = 2 * m
            total = rows_then_last(pair_of(moved[p], moved[p + 1]), s, 2)
            for d in range(2):
                rows = total[d * width : (d + 1) * width]
                if s > 0:
                    rows = own[p + d] + rows
                if s < slices - 1:
                    own[p + d] = rows
                else:
                    for g in range(groups):
                        write(g, p + d, rows[g * low : (g + 1) * low])

    def z_copy(step):
        if step < 2:
            slot = step * outer + 2 * inner
            target = outer * (1 + half) + inner * order[step]
        else:
            slot = 3
            target = order[step]
        return pltpu.make_async_remote_copy(
            src_ref=parts.at[step],
            dst_ref=slots.at[slot],
            send_sem=z_send.at[step],
            recv_sem=z_recv.at[slot],
            device_id=(target, j),
            device_id_type=MESH,
        )

    def wait_slot(slot):
        pltpu.make_async_remote_copy(
            src_ref=slots.at[slot],
            dst_ref=slots.at[slot],
            send_sem=z_send.at[0],
            recv_sem=z_recv.at[slot],
            device_id=(lax.rem(k + 1, cuts), j),
            device_id_type=MESH,
        ).wait_recv()

    def merge(step):
        @pl.when(inner == 1)
        def _():
            wait_slot(step)
            @pl.loop(0, groups)
            def _(g):
                both = parts[step, g].astype(jnp.float32) + slots[step, g].astype(jnp.float32)
                parts[step, g] = both.astype(jnp.bfloat16)
            z_copy(step).start()

    def back(i, part):
        peer = lax.rem(j + i, groups)
        rows = pl.ds(part * (width // 2), width // 2)
        return pltpu.make_async_remote_copy(
            src_ref=stage.at[peer, rows],
            dst_ref=out.at[j, rows],
            send_sem=back_send.at[part, i - 1],
            recv_sem=back_recv.at[part, i - 1],
            device_id=(k, peer),
            device_id_type=MESH,
        )

    def arrive_back(i, part):
        peer = lax.rem(j + groups - i, groups)
        rows = pl.ds(part * (width // 2), width // 2)
        return pltpu.make_async_remote_copy(
            src_ref=stage.at[peer, rows],
            dst_ref=out.at[peer, rows],
            send_sem=back_send.at[part, i - 1],
            recv_sem=back_recv.at[part, i - 1],
            device_id=(k, peer),
            device_id_type=MESH,
        )

    for step in range(cuts):
        def write(g, p, rows, step=step):
            parts[step, g, pl.ds(pl.multiple_of(p * low, low), low), :] = rows.astype(jnp.bfloat16)

        def write_last(g, p, rows):
            at = pl.ds(pl.multiple_of(p * low, low), low)
            for slot in (2, 3):
                rows = rows + slots[slot, g, at, :].astype(jnp.float32)
            stage[g, at, :] = rows.astype(jnp.bfloat16)

        for s in range(slices):
            local_in(step, s).wait()
            for i in range(1, groups):
                arrive_in(step, s, i).wait_recv()
            first_two(step, s)
            if step < cuts - 1 or s < slices - 1:
                last_two(s, 0, groups // 2, write)
            else:
                wait_slot(2)
                wait_slot(3)
                for part in range(2):
                    last_two(s, part * groups // 4, (part + 1) * groups // 4, write_last)
                    for i in range(1, groups):
                        back(i, part).start()
        if step == 2:
            z_copy(step).start()
        if step < 2:
            @pl.when(outer == 1)
            def _(step=step):
                z_copy(step).start()
        if step in (1, 2):
            merge(step - 1)

    own_copy = pltpu.make_async_copy(stage.at[j], out.at[j], own_sem)
    own_copy.start()
    for step in range(cuts):
        for s in range(slices):
            for i in range(1, groups):
                send_in(step, s, i).wait_send()
    for step in range(cuts - 1):
        z_copy(step).wait_send()
    for part in range(2):
        for i in range(1, groups):
            back(i, part).wait_send()
    for part in range(2):
        for i in range(1, groups):
            arrive_back(i, part).wait_recv()
    own_copy.wait()


def per_device_fused(stem_state, gates):
    cuts = lax.axis_size("cuts")
    groups = lax.axis_size("amp")
    slices, hidden, single, width, columns = stem_state.shape
    state = (groups, width, columns)
    bf16 = jnp.bfloat16
    result = pl.pallas_call(
        functools.partial(kernel, cuts, groups),
        out_shape=jax.ShapeDtypeStruct(state, bf16),
        in_specs=[pl.BlockSpec(memory_space=pltpu.HBM)] * 2,
        out_specs=pl.BlockSpec(memory_space=pl.ANY),
        scratch_shapes=[
            pltpu.VMEM((cuts, slices) + state, bf16),
            pltpu.VMEM(gates.shape, bf16),
            pltpu.VMEM((slices, 4, columns, columns), bf16),
            pltpu.VMEM(state, bf16),
            pltpu.VMEM((cuts - 1,) + state, bf16),
            pltpu.VMEM((4,) + state, bf16),
            pltpu.VMEM(state, jnp.float32),
            pltpu.VMEM(state, bf16),
            pltpu.SemaphoreType.DMA((cuts, slices, groups - 1)),
            pltpu.SemaphoreType.DMA((cuts, slices, groups - 1)),
            pltpu.SemaphoreType.DMA((cuts - 1,)),
            pltpu.SemaphoreType.DMA((4,)),
            pltpu.SemaphoreType.DMA((2, groups - 1)),
            pltpu.SemaphoreType.DMA((2, groups - 1)),
            pltpu.SemaphoreType.DMA((cuts, slices)),
            pltpu.SemaphoreType.DMA,
            pltpu.SemaphoreType.DMA,
        ],
        compiler_params=pltpu.CompilerParams(
            collective_id=0, has_side_effects=True, vmem_limit_bytes=60 * 1024 * 1024
        ),
    )(stem_state, gates)
    return result.astype(jnp.float32).reshape(hidden // cuts, 1, width, columns)


def per_device(stem_state, gates):
    cuts = lax.axis_size("cuts")
    groups = lax.axis_size("amp")
    hidden, width = stem_state.shape[1], stem_state.shape[3]
    if cuts == 4 and hidden == cuts * groups and width % (16 * groups) == 0 and groups % 4 == 0:
        return per_device_fused(stem_state, gates)
    return per_device_general(stem_state, gates)


def solution(mesh):
    placed = (P("cuts", None, "amp", None, None), P("cuts", None, None, None, None))
    return jax.shard_map(
        per_device,
        mesh=mesh,
        in_specs=placed,
        out_specs=P("cuts", "amp", None, None),
        check_vma=False,
    )
```

```python
import functools

import jax
import jax.numpy as jnp
from jax import lax
from jax.experimental import pallas as pl
from jax.experimental.pallas import tpu as pltpu
from jax.sharding import PartitionSpec as P

MESH = pl.DeviceIdType.MESH
BATCH = 4
LAG = 1


def block_matrix(gate):
    real_part = gate[0]
    imag_part = gate[1]
    top = jnp.concatenate([real_part.T, imag_part.T], axis=1)
    bottom = jnp.concatenate([-imag_part.T, real_part.T], axis=1)
    return jnp.concatenate([top, bottom], axis=0)


def on_rows(values, real_gates, imag_gates):
    width = values.shape[-1] // 2
    first_term = jnp.einsum(
        "ska,shgac->shgkc", real_gates, values, preferred_element_type=jnp.float32
    )
    second_term = jnp.einsum(
        "ska,shgac->shgkc", imag_gates, values, preferred_element_type=jnp.float32
    )
    real_out = first_term[..., :width] - second_term[..., width:]
    imag_out = first_term[..., width:] + second_term[..., :width]
    return jnp.concatenate([real_out, imag_out], axis=-1)


def on_last(values, matrices):
    return jnp.einsum("shgac,scd->shgad", values, matrices, preferred_element_type=jnp.float32)


def per_device_general(stem_state, gates):
    groups = lax.axis_size("amp")
    slice_count, hidden, single, width, columns = stem_state.shape
    low = width // groups
    first = on_rows(stem_state, gates[:, 0, 0], gates[:, 0, 1]).astype(jnp.bfloat16)
    second_matrix = jax.vmap(block_matrix)(gates[:, 1])
    second = on_last(first, second_matrix).astype(jnp.bfloat16)
    split_state = second.reshape(slice_count, hidden, 1, groups, low, columns)
    last_matrix = jax.vmap(block_matrix)(gates[:, 3])
    pieces = lax.all_to_all(split_state, "amp", split_axis=3, concat_axis=2, tiled=True)
    count = pieces.shape[1]
    merged = pieces.reshape(slice_count, count, 1, width, columns)
    third = on_rows(merged, gates[:, 2, 0], gates[:, 2, 1]).astype(jnp.bfloat16)
    fourth = on_last(third, last_matrix).reshape(slice_count, count, width, columns)
    total = jnp.sum(fourth, axis=0)
    summed = lax.psum_scatter(total, "cuts", scatter_dimension=0, tiled=True)
    share = summed.shape[0]
    outgoing = summed.reshape(share, groups, 1, low, columns)
    owned = lax.all_to_all(outgoing, "amp", split_axis=1, concat_axis=2, tiled=True)
    return owned.reshape(share, 1, width, columns)


def dot(a, b):
    return jnp.dot(a, b, preferred_element_type=jnp.float32)


def pair_of(first, second):
    half = first.shape[1] // 2
    return jnp.concatenate(
        [
            jnp.concatenate([first[:, :half], second[:, :half]], axis=1),
            jnp.concatenate([first[:, half:], second[:, half:]], axis=1),
        ],
        axis=0,
    )


def kernel(cuts, groups, stem, gates, out, stem_buf, gate_buf, blocks, second, land, parts, slots,
           stage, in_send, in_recv, z_send, z_recv, back_send, back_recv, stem_sem, own_sem,
           gate_sem, done_sem):
    slices, hidden, single, width, columns = stem.shape
    low = width // groups
    share = hidden // cuts
    subs = share // BATCH
    k = lax.axis_index("cuts")
    j = lax.axis_index("amp")
    mine = pl.ds(pl.multiple_of(j * low, low), low)

    barrier = pltpu.get_barrier_semaphore()
    for i in range(1, groups):
        pl.semaphore_signal(barrier, inc=1, device_id=(k, lax.rem(j + i, groups)), device_id_type=MESH)
    for i in range(1, cuts):
        pl.semaphore_signal(barrier, inc=1, device_id=(lax.rem(k + i, cuts), j), device_id_type=MESH)
    gate_copy = pltpu.make_async_copy(gates, gate_buf, gate_sem)
    gate_copy.start()

    half = k // 2
    inner = (k * (3 - k)) // 2
    outer = 1 - inner
    order = [3 * (1 - half), 2 - half, 4 * half + 1 - k, k]
    steps = [(t, u) for t in range(cuts) for u in range(subs)]

    def load(n):
        t, u = steps[n]
        return pltpu.make_async_copy(
            stem.at[:, pl.ds(order[t] * share + u * BATCH, BATCH), 0], stem_buf.at[n], stem_sem.at[n]
        )

    for n in range(len(steps)):
        load(n).start()

    gate_copy.wait()
    for s in range(slices):
        for n in range(4):
            re = gate_buf[s, n, 0]
            im = gate_buf[s, n, 1]
            if n % 2 == 0:
                blocks[s, n, :width, :width] = re
                blocks[s, n, :width, width:] = -im
                blocks[s, n, width:, :width] = im
                blocks[s, n, width:, width:] = re
            else:
                re = re.T
                im = im.T
                blocks[s, n, :width, :width] = re
                blocks[s, n, :width, width:] = im
                blocks[s, n, width:, :width] = -im
                blocks[s, n, width:, width:] = re

    def rows_then_last(pair, s, n):
        mid = dot(blocks[s, n], pair).astype(jnp.bfloat16)
        turned = jnp.concatenate(
            [
                jnp.concatenate([mid[:width, :width], mid[width:, :width]], axis=1),
                jnp.concatenate([mid[:width, width:], mid[width:, width:]], axis=1),
            ],
            axis=0,
        )
        return dot(turned, blocks[s, n + 1])

    def rows_of(peer):
        return pl.ds(pl.multiple_of(peer * low, low), low)

    def send_in(n, i):
        peer = lax.rem(j + i, groups)
        return pltpu.make_async_remote_copy(
            src_ref=second.at[n, :, :, rows_of(peer)],
            dst_ref=land.at[n, :, :, mine],
            send_sem=in_send.at[n, i - 1],
            recv_sem=in_recv.at[n, i - 1],
            device_id=(k, peer),
            device_id_type=MESH,
        )

    def arrive_in(n, i):
        peer = lax.rem(j + groups - i, groups)
        return pltpu.make_async_remote_copy(
            src_ref=land.at[n, :, :, rows_of(peer)],
            dst_ref=land.at[n, :, :, rows_of(peer)],
            send_sem=in_send.at[n, i - 1],
            recv_sem=in_recv.at[n, i - 1],
            device_id=(k, peer),
            device_id_type=MESH,
        )

    def keep(n):
        return pltpu.make_async_copy(
            second.at[n, :, :, mine], land.at[n, :, :, mine], own_sem.at[n]
        )

    for n in range(len(steps)):
        load(n).wait()

        @pl.loop(0, BATCH // 2)
        def _(m, n=n):
            h = 2 * m
            for s in range(slices):
                res = rows_then_last(pair_of(stem_buf[n, s, h], stem_buf[n, s, h + 1]), s, 0)
                res = res.astype(jnp.bfloat16)
                second[n, s, h] = res[:width]
                second[n, s, h + 1] = res[width:]

        if n == 0:
            pl.semaphore_wait(barrier, groups - 1 + cuts - 1)
        for i in range(1, groups):
            send_in(n, i).start()
        keep(n).start()

    def z_copy(t, u):
        if t < 2:
            slot = t * outer + 2 * inner
            target = outer * (1 + half) + inner * order[t]
        else:
            slot = 3
            target = order[t]
        return pltpu.make_async_remote_copy(
            src_ref=parts.at[t, u],
            dst_ref=slots.at[slot, u],
            send_sem=z_send.at[t, u],
            recv_sem=z_recv.at[slot, u],
            device_id=(target, j),
            device_id_type=MESH,
        )

    def wait_slot(slot, u):
        pltpu.make_async_remote_copy(
            src_ref=slots.at[slot, u],
            dst_ref=slots.at[slot, u],
            send_sem=z_send.at[0, u],
            recv_sem=z_recv.at[slot, u],
            device_id=(lax.rem(k + 1, cuts), j),
            device_id_type=MESH,
        ).wait_recv()

    def merge(t, u):
        @pl.when(inner == 1)
        def _():
            wait_slot(t, u)

            @pl.loop(0, BATCH)
            def _(h):
                both = parts[t, u, h].astype(jnp.float32) + slots[t, u, h].astype(jnp.float32)
                parts[t, u, h] = both.astype(jnp.bfloat16)

            z_copy(t, u).start()

    def back(i, u):
        peer = lax.rem(j + i, groups)
        return pltpu.make_async_remote_copy(
            src_ref=stage.at[u, :, rows_of(peer)],
            dst_ref=out.at[pl.ds(u * BATCH, BATCH), mine],
            send_sem=back_send.at[u, i - 1],
            recv_sem=back_recv.at[u, i - 1],
            device_id=(k, peer),
            device_id_type=MESH,
        )

    def arrive_back(i, u):
        peer = lax.rem(j + groups - i, groups)
        return pltpu.make_async_remote_copy(
            src_ref=stage.at[u, :, rows_of(peer)],
            dst_ref=out.at[pl.ds(u * BATCH, BATCH), rows_of(peer)],
            send_sem=back_send.at[u, i - 1],
            recv_sem=back_recv.at[u, i - 1],
            device_id=(k, peer),
            device_id_type=MESH,
        )

    def keep_back(u):
        return pltpu.make_async_copy(
            stage.at[u, :, mine], out.at[pl.ds(u * BATCH, BATCH), mine], done_sem.at[u]
        )

    for n, (t, u) in enumerate(steps):
        keep(n).wait()
        for i in range(1, groups):
            arrive_in(n, i).wait_recv()
        if t == cuts - 1:
            wait_slot(2, u)
            wait_slot(3, u)

        @pl.loop(0, BATCH // 2)
        def _(m, n=n, t=t, u=u):
            h = 2 * m
            total = None
            for s in range(slices):
                term = rows_then_last(pair_of(land[n, s, h], land[n, s, h + 1]), s, 2)
                total = term if total is None else total + term
            for d in range(2):
                rows = total[d * width : (d + 1) * width]
                if t < cuts - 1:
                    parts[t, u, h + d] = rows.astype(jnp.bfloat16)
                else:
                    for slot in (2, 3):
                        rows = rows + slots[slot, u, h + d].astype(jnp.float32)
                    stage[u, h + d] = rows.astype(jnp.bfloat16)

        if t < 2:
            @pl.when(outer == 1)
            def _(t=t, u=u):
                z_copy(t, u).start()
        elif t == 2:
            z_copy(t, u).start()
        else:
            for i in range(1, groups):
                back(i, u).start()
            keep_back(u).start()
        if n >= LAG and steps[n - LAG][0] < 2:
            merge(*steps[n - LAG])

    for n in range(len(steps)):
        for i in range(1, groups):
            send_in(n, i).wait_send()
    for t in range(cuts - 1):
        for u in range(subs):
            z_copy(t, u).wait_send()
    for u in range(subs):
        keep_back(u).wait()
        for i in range(1, groups):
            back(i, u).wait_send()
    for u in range(subs):
        for i in range(1, groups):
            arrive_back(i, u).wait_recv()


def per_device_fused(stem_state, gates):
    cuts = lax.axis_size("cuts")
    groups = lax.axis_size("amp")
    slices, hidden, single, width, columns = stem_state.shape
    share = hidden // cuts
    subs = share // BATCH
    steps = cuts * subs
    bf16 = jnp.bfloat16
    states = (steps, slices, BATCH, width, columns)
    sums = (subs, BATCH, width, columns)
    result = pl.pallas_call(
        functools.partial(kernel, cuts, groups),
        out_shape=jax.ShapeDtypeStruct((share, width, columns), bf16),
        in_specs=[pl.BlockSpec(memory_space=pltpu.HBM)] * 2,
        out_specs=pl.BlockSpec(memory_space=pl.ANY),
        scratch_shapes=[
            pltpu.VMEM(states, bf16),
            pltpu.VMEM(gates.shape, bf16),
            pltpu.VMEM((slices, 4, columns, columns), bf16),
            pltpu.VMEM(states, bf16),
            pltpu.VMEM(states, bf16),
            pltpu.VMEM((cuts - 1,) + sums, bf16),
            pltpu.VMEM((4,) + sums, bf16),
            pltpu.VMEM(sums, bf16),
            pltpu.SemaphoreType.DMA((steps, groups - 1)),
            pltpu.SemaphoreType.DMA((steps, groups - 1)),
            pltpu.SemaphoreType.DMA((cuts - 1, subs)),
            pltpu.SemaphoreType.DMA((4, subs)),
            pltpu.SemaphoreType.DMA((subs, groups - 1)),
            pltpu.SemaphoreType.DMA((subs, groups - 1)),
            pltpu.SemaphoreType.DMA((steps,)),
            pltpu.SemaphoreType.DMA((steps,)),
            pltpu.SemaphoreType.DMA,
            pltpu.SemaphoreType.DMA((subs,)),
        ],
        compiler_params=pltpu.CompilerParams(
            collective_id=0, has_side_effects=True, vmem_limit_bytes=60 * 1024 * 1024
        ),
    )(stem_state, gates)
    return result.astype(jnp.float32).reshape(share, 1, width, columns)


def per_device(stem_state, gates):
    cuts = lax.axis_size("cuts")
    groups = lax.axis_size("amp")
    hidden, width = stem_state.shape[1], stem_state.shape[3]
    if cuts == 4 and hidden % (cuts * BATCH) == 0 and width % (16 * groups) == 0:
        return per_device_fused(stem_state, gates)
    return per_device_general(stem_state, gates)


def solution(mesh):
    placed = (P("cuts", None, "amp", None, None), P("cuts", None, None, None, None))
    return jax.shard_map(
        per_device,
        mesh=mesh,
        in_specs=placed,
        out_specs=P("cuts", "amp", None, None),
        check_vma=False,
    )
```

```python
import functools

import jax
import jax.numpy as jnp
from jax import lax
from jax.experimental import pallas as pl
from jax.experimental.pallas import tpu as pltpu
from jax.sharding import PartitionSpec as P

MESH = pl.DeviceIdType.MESH
BATCH = 4
FIRST = True
FINAL = False


def block_matrix(gate):
    real_part = gate[0]
    imag_part = gate[1]
    top = jnp.concatenate([real_part.T, imag_part.T], axis=1)
    bottom = jnp.concatenate([-imag_part.T, real_part.T], axis=1)
    return jnp.concatenate([top, bottom], axis=0)


def on_rows(values, real_gates, imag_gates):
    width = values.shape[-1] // 2
    first_term = jnp.einsum(
        "ska,shgac->shgkc", real_gates, values, preferred_element_type=jnp.float32
    )
    second_term = jnp.einsum(
        "ska,shgac->shgkc", imag_gates, values, preferred_element_type=jnp.float32
    )
    real_out = first_term[..., :width] - second_term[..., width:]
    imag_out = first_term[..., width:] + second_term[..., :width]
    return jnp.concatenate([real_out, imag_out], axis=-1)


def on_last(values, matrices):
    return jnp.einsum("shgac,scd->shgad", values, matrices, preferred_element_type=jnp.float32)


def per_device_general(stem_state, gates):
    groups = lax.axis_size("amp")
    slice_count, hidden, single, width, columns = stem_state.shape
    low = width // groups
    first = on_rows(stem_state, gates[:, 0, 0], gates[:, 0, 1]).astype(jnp.bfloat16)
    second_matrix = jax.vmap(block_matrix)(gates[:, 1])
    second = on_last(first, second_matrix).astype(jnp.bfloat16)
    split_state = second.reshape(slice_count, hidden, 1, groups, low, columns)
    last_matrix = jax.vmap(block_matrix)(gates[:, 3])
    pieces = lax.all_to_all(split_state, "amp", split_axis=3, concat_axis=2, tiled=True)
    count = pieces.shape[1]
    merged = pieces.reshape(slice_count, count, 1, width, columns)
    third = on_rows(merged, gates[:, 2, 0], gates[:, 2, 1]).astype(jnp.bfloat16)
    fourth = on_last(third, last_matrix).reshape(slice_count, count, width, columns)
    total = jnp.sum(fourth, axis=0)
    summed = lax.psum_scatter(total, "cuts", scatter_dimension=0, tiled=True)
    share = summed.shape[0]
    outgoing = summed.reshape(share, groups, 1, low, columns)
    owned = lax.all_to_all(outgoing, "amp", split_axis=1, concat_axis=2, tiled=True)
    return owned.reshape(share, 1, width, columns)


def dot(a, b):
    return jnp.dot(a, b, preferred_element_type=jnp.float32)


def pair_of(first, second):
    half = first.shape[1] // 2
    return jnp.concatenate(
        [
            jnp.concatenate([first[:, :half], second[:, :half]], axis=1),
            jnp.concatenate([first[:, half:], second[:, half:]], axis=1),
        ],
        axis=0,
    )


def kernel(cuts, groups, stem, gates, out, stem_buf, gate_buf, blocks, second, land, parts, slots,
           stage, in_send, in_recv, z_send, z_recv, back_send, back_recv, stem_sem, own_sem,
           gate_sem, done_sem):
    slices, hidden, single, width, columns = stem.shape
    low = width // groups
    share = hidden // cuts
    subs = share // BATCH
    k = lax.axis_index("cuts")
    j = lax.axis_index("amp")
    mine = pl.ds(pl.multiple_of(j * low, low), low)

    barrier = pltpu.get_barrier_semaphore()
    for i in range(1, groups):
        pl.semaphore_signal(barrier, inc=1, device_id=(k, lax.rem(j + i, groups)), device_id_type=MESH)
    for i in range(1, cuts):
        pl.semaphore_signal(barrier, inc=1, device_id=(lax.rem(k + i, cuts), j), device_id_type=MESH)
    gate_copy = pltpu.make_async_copy(gates, gate_buf, gate_sem)
    gate_copy.start()

    half = k // 2
    inner = (k * (3 - k)) // 2
    outer = 1 - inner
    order = [3 * (1 - half), 2 - half, 4 * half + 1 - k, k]
    steps = steps_of(cuts, share)

    def load(n):
        t, at, size = steps[n]
        return pltpu.make_async_copy(
            stem.at[:, pl.ds(order[t] * share + at, size), 0],
            stem_buf.at[t, :, pl.ds(at, size)],
            stem_sem.at[n],
        )

    for n in range(len(steps)):
        load(n).start()

    def prepare(n):
        for s in range(slices):
            re = gate_buf[s, n, 0]
            im = gate_buf[s, n, 1]
            if n % 2 == 0:
                blocks[s, n, :width, :width] = re
                blocks[s, n, :width, width:] = -im
                blocks[s, n, width:, :width] = im
                blocks[s, n, width:, width:] = re
            else:
                re = re.T
                im = im.T
                blocks[s, n, :width, :width] = re
                blocks[s, n, :width, width:] = im
                blocks[s, n, width:, :width] = -im
                blocks[s, n, width:, width:] = re

    gate_copy.wait()
    prepare(0)
    prepare(1)

    def rows_then_last(pair, s, n):
        mid = dot(blocks[s, n], pair).astype(jnp.bfloat16)
        turned = jnp.concatenate(
            [
                jnp.concatenate([mid[:width, :width], mid[width:, :width]], axis=1),
                jnp.concatenate([mid[:width, width:], mid[width:, width:]], axis=1),
            ],
            axis=0,
        )
        return dot(turned, blocks[s, n + 1])

    def rows_of(peer):
        return pl.ds(pl.multiple_of(peer * low, low), low)

    def part_of(ref, n, rows):
        t, at, size = steps[n]
        return ref.at[t, :, pl.ds(at, size), rows]

    def send_in(n, i):
        peer = lax.rem(j + i, groups)
        return pltpu.make_async_remote_copy(
            src_ref=part_of(second, n, rows_of(peer)),
            dst_ref=part_of(land, n, mine),
            send_sem=in_send.at[n, i - 1],
            recv_sem=in_recv.at[n, i - 1],
            device_id=(k, peer),
            device_id_type=MESH,
        )

    def arrive_in(n, i):
        peer = lax.rem(j + groups - i, groups)
        return pltpu.make_async_remote_copy(
            src_ref=part_of(land, n, rows_of(peer)),
            dst_ref=part_of(land, n, rows_of(peer)),
            send_sem=in_send.at[n, i - 1],
            recv_sem=in_recv.at[n, i - 1],
            device_id=(k, peer),
            device_id_type=MESH,
        )

    def keep(n):
        return pltpu.make_async_copy(
            part_of(second, n, mine), part_of(land, n, mine), own_sem.at[n]
        )

    for n, (t, at, size) in enumerate(steps):
        load(n).wait()

        @pl.loop(at // 2, (at + size) // 2)
        def _(m, t=t):
            h = 2 * m
            for s in range(slices):
                res = rows_then_last(pair_of(stem_buf[t, s, h], stem_buf[t, s, h + 1]), s, 0)
                res = res.astype(jnp.bfloat16)
                second[t, s, h] = res[:width]
                second[t, s, h + 1] = res[width:]

        if n == 0:
            pl.semaphore_wait(barrier, groups - 1 + cuts - 1)
        for i in range(1, groups):
            send_in(n, i).start()
        keep(n).start()
        if n == 0:
            prepare(2)
            prepare(3)

    def z_copy(t, u):
        if t < 2:
            slot = t * outer + 2 * inner
            target = outer * (1 + half) + inner * order[t]
        else:
            slot = 3
            target = order[t]
        return pltpu.make_async_remote_copy(
            src_ref=parts.at[t, u],
            dst_ref=slots.at[slot, u],
            send_sem=z_send.at[t, u],
            recv_sem=z_recv.at[slot, u],
            device_id=(target, j),
            device_id_type=MESH,
        )

    def wait_slot(slot, u):
        pltpu.make_async_remote_copy(
            src_ref=slots.at[slot, u],
            dst_ref=slots.at[slot, u],
            send_sem=z_send.at[0, u],
            recv_sem=z_recv.at[slot, u],
            device_id=(lax.rem(k + 1, cuts), j),
            device_id_type=MESH,
        ).wait_recv()

    def merge(t, u):
        @pl.when(inner == 1)
        def _():
            wait_slot(t, u)

            @pl.loop(0, BATCH)
            def _(h):
                both = parts[t, u, h].astype(jnp.float32) + slots[t, u, h].astype(jnp.float32)
                parts[t, u, h] = both.astype(jnp.bfloat16)

            z_copy(t, u).start()

    last = [n for n in range(len(steps)) if steps[n][0] == cuts - 1]

    def back(i, v):
        at, size = steps[last[v]][1:]
        peer = lax.rem(j + i, groups)
        return pltpu.make_async_remote_copy(
            src_ref=stage.at[pl.ds(at, size), rows_of(peer)],
            dst_ref=out.at[pl.ds(at, size), mine],
            send_sem=back_send.at[v, i - 1],
            recv_sem=back_recv.at[v, i - 1],
            device_id=(k, peer),
            device_id_type=MESH,
        )

    def arrive_back(i, v):
        at, size = steps[last[v]][1:]
        peer = lax.rem(j + groups - i, groups)
        return pltpu.make_async_remote_copy(
            src_ref=stage.at[pl.ds(at, size), rows_of(peer)],
            dst_ref=out.at[pl.ds(at, size), rows_of(peer)],
            send_sem=back_send.at[v, i - 1],
            recv_sem=back_recv.at[v, i - 1],
            device_id=(k, peer),
            device_id_type=MESH,
        )

    def keep_back(v):
        at, size = steps[last[v]][1:]
        return pltpu.make_async_copy(
            stage.at[pl.ds(at, size), mine], out.at[pl.ds(at, size), mine], done_sem.at[v]
        )

    waiting = []
    for n, (t, at, size) in enumerate(steps):
        keep(n).wait()
        for i in range(1, groups):
            arrive_in(n, i).wait_recv()
        if t == cuts - 1 and at % BATCH == 0:
            wait_slot(2, at // BATCH)
            wait_slot(3, at // BATCH)

        @pl.loop(at // 2, (at + size) // 2)
        def _(m, t=t, u=at // BATCH):
            h = 2 * m
            total = None
            for s in range(slices):
                term = rows_then_last(pair_of(land[t, s, h], land[t, s, h + 1]), s, 2)
                total = term if total is None else total + term
            for d in range(2):
                rows = total[d * width : (d + 1) * width]
                if t < cuts - 1:
                    parts[t, u, h + d - u * BATCH] = rows.astype(jnp.bfloat16)
                else:
                    for slot in (2, 3):
                        rows = rows + slots[slot, u, h + d - u * BATCH].astype(jnp.float32)
                    stage[h + d] = rows.astype(jnp.bfloat16)

        if t == cuts - 1:
            v = last.index(n)
            for i in range(1, groups):
                back(i, v).start()
            keep_back(v).start()
        elif (at + size) % BATCH == 0:
            u = at // BATCH
            if t < 2:
                @pl.when(outer == 1)
                def _(t=t, u=u):
                    z_copy(t, u).start()
            else:
                z_copy(t, u).start()
            if waiting:
                merge(*waiting.pop())
            if t < 2:
                waiting.append((t, u))

    for n in range(len(steps)):
        for i in range(1, groups):
            send_in(n, i).wait_send()
    for t in range(cuts - 1):
        for u in range(subs):
            z_copy(t, u).wait_send()
    for v in range(len(last)):
        keep_back(v).wait()
        for i in range(1, groups):
            back(i, v).wait_send()
    for v in range(len(last)):
        for i in range(1, groups):
            arrive_back(i, v).wait_recv()


def steps_of(cuts, share):
    sizes = [[BATCH] * (share // BATCH) for t in range(cuts)]
    if FIRST:
        sizes[0][:1] = [BATCH // 2] * 2
    if FINAL:
        sizes[-1][-1:] = [BATCH // 2] * 2
    return [(t, sum(row[:c]), row[c]) for t, row in enumerate(sizes) for c in range(len(row))]


def per_device_fused(stem_state, gates):
    cuts = lax.axis_size("cuts")
    groups = lax.axis_size("amp")
    slices, hidden, single, width, columns = stem_state.shape
    share = hidden // cuts
    subs = share // BATCH
    steps = len(steps_of(cuts, share))
    last = len([step for step in steps_of(cuts, share) if step[0] == cuts - 1])
    bf16 = jnp.bfloat16
    states = (cuts, slices, share, width, columns)
    sums = (subs, BATCH, width, columns)
    result = pl.pallas_call(
        functools.partial(kernel, cuts, groups),
        out_shape=jax.ShapeDtypeStruct((share, width, columns), bf16),
        in_specs=[pl.BlockSpec(memory_space=pltpu.HBM)] * 2,
        out_specs=pl.BlockSpec(memory_space=pl.ANY),
        scratch_shapes=[
            pltpu.VMEM(states, bf16),
            pltpu.VMEM(gates.shape, bf16),
            pltpu.VMEM((slices, 4, columns, columns), bf16),
            pltpu.VMEM(states, bf16),
            pltpu.VMEM(states, bf16),
            pltpu.VMEM((cuts - 1,) + sums, bf16),
            pltpu.VMEM((4,) + sums, bf16),
            pltpu.VMEM((share, width, columns), bf16),
            pltpu.SemaphoreType.DMA((steps, groups - 1)),
            pltpu.SemaphoreType.DMA((steps, groups - 1)),
            pltpu.SemaphoreType.DMA((cuts - 1, subs)),
            pltpu.SemaphoreType.DMA((4, subs)),
            pltpu.SemaphoreType.DMA((last, groups - 1)),
            pltpu.SemaphoreType.DMA((last, groups - 1)),
            pltpu.SemaphoreType.DMA((steps,)),
            pltpu.SemaphoreType.DMA((steps,)),
            pltpu.SemaphoreType.DMA,
            pltpu.SemaphoreType.DMA((last,)),
        ],
        compiler_params=pltpu.CompilerParams(
            collective_id=0, has_side_effects=True, vmem_limit_bytes=60 * 1024 * 1024
        ),
    )(stem_state, gates)
    return result.astype(jnp.float32).reshape(share, 1, width, columns)


def per_device(stem_state, gates):
    cuts = lax.axis_size("cuts")
    groups = lax.axis_size("amp")
    hidden, width = stem_state.shape[1], stem_state.shape[3]
    if cuts == 4 and hidden % (cuts * BATCH) == 0 and width % (16 * groups) == 0:
        return per_device_fused(stem_state, gates)
    return per_device_general(stem_state, gates)


def solution(mesh):
    placed = (P("cuts", None, "amp", None, None), P("cuts", None, None, None, None))
    return jax.shard_map(
        per_device,
        mesh=mesh,
        in_specs=placed,
        out_specs=P("cuts", "amp", None, None),
        check_vma=False,
    )
```
